768 devices in a mesh: comp: 8 (over x, core), tile: 96 (over y, z).
Axes of the slice: x: 4, y: 8, z: 12, core: 2. Of those that a mesh axis runs over, the one named last changes fastest.
Arguments:
- fields: float32 [80, 3145728], P(None, ('comp', 'tile')), may hold values from -6 to 6
- neighbour_offset: int32 [8, 3145728], P(None, ('comp', 'tile')), may hold values from -256 to 256
- neighbour_weight: float32 [8, 3145728], P(None, ('comp', 'tile')), may hold values from 0.02 to 0.115
- vertical_mix: float32 [8, 80, 80], P('comp'), may hold values from -0.3125 to 0.3125
- remap_source: int32 [2304, 1024], P(('comp', 'tile')), may hold values from 0 to 4095
- remap_weight: float32 [2304, 1024], P(('comp', 'tile')), may hold values from 0.1 to 1
- remap_count: int32 [768, 3], P(('comp', 'tile')), may hold values from 819 to 1024, as said below
- remap_target: int32 [2304, 1024], P(('comp', 'tile')), may hold values from 0 to 4095
Outputs:
- new_fields: float32 [80, 3145728], P(None, ('comp', 'tile'))
- surface_flux: float32 [16, 3145728], P(None, ('comp', 'tile'))
The draws below stay inside these ranges and needn't reach their ends.
Inputs may be any that keep to these rules, and one draw needn't show every extreme that they name: `remap_count`: some entry equals 1024, in a row block of an atmosphere device whose destination is an ocean comp index.
All inputs are finite; a program needn't handle non-finite values.
Results may differ from the reference program's by a relative error of at most 0.0003.
Values sent between devices are 32-bit elements; how exact they have to be, the bound alone decides.
A program may use at most 32 MiB of HBM per device.

```python
import math
import jax
import jax.numpy as jnp
from jax import lax

ROWS = 80
SURF = 16
NBR = 8
CELLS = 4096
HALO = 256
SLOTS = 1024
BAND = 393216
TOTAL = 3145728
ATM_COMP = 6
STRIDE = 2
N_COMP = 8
N_TILE = 96
DEVICES = 768


def draw_remap_count(key, part):
    key = jax.random.fold_in(key, 11)
    first, second = jax.random.split(key, 2)
    tiles = DEVICES // N_COMP
    counts = jax.random.randint(first, (DEVICES, 3), 4 * SLOTS // 5, SLOTS + 1)
    device_row = jax.random.randint(second, (), 0, N_COMP // 4 * tiles)
    counts = counts.at[device_row, 2].set(SLOTS)
    return counts.astype(jnp.int32)


def with_ends(array, rng, low, largest):
    shape = array.shape
    index_at = [jax.random.randint(jax.random.fold_in(rng, axis), (), 0, shape[axis]) for axis in range(len(shape))]
    array = array.at[tuple(index_at)].set(low)
    longest = shape.index(max(shape))
    index_at[longest] = (index_at[longest] + 1) % shape[longest]
    return array.at[tuple(index_at)].set(largest)


def block_levels(rng, extent, cuts, least, top_value):
    factor_of, own = 1.0, jax.random.fold_in(rng, 6)
    for dim, blocks in cuts:
        heights = jnp.exp(jax.random.uniform(jax.random.fold_in(own, dim), (blocks,), jnp.float32, least / len(cuts), top_value / len(cuts)))
        factor_of = factor_of * jnp.repeat(heights, extent[dim] // blocks).reshape([-1 if axis == dim else 1 for axis in range(len(extent))])
    return factor_of


def normal_values(key, extent, spread, limit, shards=(), held_as=jnp.bfloat16):
    entries = spread * jax.random.normal(key, extent, jnp.float32)
    if shards:
        entries = entries * block_levels(key, extent, shards, -0.22, 0.18)
    return jnp.clip(entries, -limit, limit).astype(held_as)


def setup_inputs(seed: int = 0) -> dict:
    seeds = jax.random.split(jax.random.key(seed), 9)
    return {
        "fields": normal_values(seeds[0], (ROWS, TOTAL), 1.0, 6.0, ((1, 768),), jnp.float32),
        "neighbour_offset": with_ends(jax.random.randint(seeds[1], (NBR, TOTAL), 0 - HALO, HALO + 1), jax.random.fold_in(seeds[1], 1), 0 - HALO, HALO).astype(jnp.int32),
        "neighbour_weight": jnp.clip(jnp.exp(math.log(0.115) - 1.7491999 * jax.random.uniform(seeds[2], (NBR, TOTAL), jnp.float32) ** block_levels(seeds[2], (NBR, TOTAL), ((1, 768),), -0.2, 0.2)), 0.02, 0.115),
        "vertical_mix": normal_values(seeds[3], (N_COMP, ROWS, ROWS), (4 * ROWS) ** -0.5, 0.3125, ((0, 8),), jnp.float32),
        "remap_source": with_ends(jax.random.randint(seeds[4], (3 * TOTAL // CELLS, SLOTS), 0, CELLS), jax.random.fold_in(seeds[4], 1), 0, CELLS - 1).astype(jnp.int32),
        "remap_weight": jnp.clip(jnp.exp(math.log(1.0) - 2.3025851 * jax.random.uniform(seeds[5], (3 * TOTAL // CELLS, SLOTS), jnp.float32) ** block_levels(seeds[5], (3 * TOTAL // CELLS, SLOTS), ((0, 768),), -0.2, 0.2)), 0.1, 1.0),
        "remap_count": draw_remap_count(jax.random.fold_in(seeds[8], 71), 0),
        "remap_target": with_ends(jax.random.randint(seeds[7], (3 * TOTAL // CELLS, SLOTS), 0, CELLS), jax.random.fold_in(seeds[7], 1), 0, CELLS - 1).astype(jnp.int32),
    }


def advance_band(block, offsets, weights, vertical):
    length = block.shape[1]
    position = jnp.arange(length, dtype=jnp.int32)
    tendency = jnp.zeros_like(block)
    for neighbour in range(NBR):
        indices = jnp.mod(position + offsets[neighbour], length).astype(jnp.int32)
        tendency = tendency + weights[neighbour] * (jnp.take(block, indices, axis=1) - block)
    moved = block + tendency
    return moved + jnp.dot(vertical, moved, precision=lax.Precision.HIGHEST)


def reference(fields, neighbour_offset, neighbour_weight, vertical_mix, remap_source, remap_weight, remap_count, remap_target):
    bands = fields.reshape(ROWS, N_COMP, BAND).transpose(1, 0, 2)
    offsets = neighbour_offset.reshape(NBR, N_COMP, BAND).transpose(1, 0, 2)
    weights = neighbour_weight.reshape(NBR, N_COMP, BAND).transpose(1, 0, 2)

    def one_band(packed):
        block, offs_band, wts_band, vertical = packed
        block = advance_band(block, offs_band, wts_band, vertical)
        block = advance_band(block, offs_band, wts_band, vertical)
        return block

    finished = lax.map(one_band, (bands, offsets, weights, vertical_mix))
    new_fields = finished.transpose(1, 0, 2).reshape(ROWS, TOTAL)

    surface = finished[:, :SURF].reshape(N_COMP, SURF, N_TILE, CELLS).transpose(0, 2, 1, 3)
    source = remap_source.reshape(N_COMP, N_TILE, 3, SLOTS)
    weight = remap_weight.reshape(N_COMP, N_TILE, 3, SLOTS)
    count = remap_count.reshape(N_COMP, N_TILE, 3)
    target = remap_target.reshape(N_COMP, N_TILE, 3, SLOTS)

    def pack(surface_block, source_block, weight_block, count_block, sender):
        picked = jnp.take(surface_block, source_block.reshape(-1), axis=1).reshape(SURF, 3, SLOTS)
        dest = jnp.mod(sender + jnp.arange(1, 4, dtype=jnp.int32) * STRIDE, N_COMP)
        crosses = (dest < ATM_COMP) != (sender < ATM_COMP)
        active = crosses[:, None] & (jnp.arange(SLOTS, dtype=jnp.int32)[None, :] < count_block[:, None])
        return jnp.where(active[None], weight_block[None] * picked, jnp.float32(0.0))

    senders = jnp.arange(N_COMP, dtype=jnp.int32)
    packets = jax.vmap(jax.vmap(pack, in_axes=(0, 0, 0, 0, None)), in_axes=(0, 0, 0, 0, 0))(surface, source, weight, count, senders)
    arrived = [jnp.roll(packets[:, :, :, step], (step + 1) * STRIDE, axis=0) for step in range(3)]
    received = jnp.stack(arrived, axis=3)

    def land(arrival, target_block):
        empty = jnp.zeros((SURF, CELLS), jnp.float32)
        return empty.at[:, target_block.reshape(-1)].add(arrival.reshape(SURF, -1))

    flux = jax.vmap(jax.vmap(land))(received, target)
    surface_flux = flux.transpose(2, 0, 1, 3).reshape(SURF, TOTAL)
    return new_fields, surface_flux
```

```python
import jax
import jax.numpy as jnp
from jax import lax
from jax.experimental import pallas as pl
from jax.experimental.pallas import tpu as pltpu
from jax.sharding import PartitionSpec as P

ROWS = 80
SURF = 16
REST = ROWS - SURF
NBR = 8
CELLS = 4096
HALO = 256
SLOTS = 1024
TILE = 128
BLOCK = 256
WINDOW = TILE + 2 * HALO
SPAN = BLOCK + 2 * HALO
NEAR = CELLS + 2 * HALO
WIDE = CELLS + 4 * HALO
OCEAN_X = 3
BF16 = jnp.bfloat16
F32 = jnp.float32
MESH = pl.DeviceIdType.MESH


def halves(value):
    high = value.astype(BF16)
    return high, (value - high.astype(F32)).astype(BF16)


def put_halves(ref, column, width, value):
    high, low = halves(value)
    columns = pl.ds(column, width)
    ref[0:SURF, columns] = high[:SURF]
    ref[SURF : 2 * SURF, columns] = low[:SURF]
    ref[2 * SURF : 2 * SURF + REST, columns] = high[SURF:]
    ref[2 * SURF + REST :, columns] = low[SURF:]


def row_of(ref, row, columns):
    second_or_third = jnp.where(row == 1, ref[1:2, columns], ref[2:3, columns])
    return jnp.where(row == 0, ref[0:1, columns], second_or_third)


def build_tile(tile, offset_ref, weight_ref, high_ref, low_ref):
    columns = pl.ds(pl.multiple_of(tile * TILE, TILE), TILE)
    offset = offset_ref[:, columns]
    weight = weight_ref[:, columns]
    total = weight
    for shift in range(1, NBR):
        same = pltpu.roll(offset, shift, 0) == offset
        total = total + jnp.where(same, pltpu.roll(weight, shift, 0), 0.0)
    place = offset + HALO + lax.broadcasted_iota(jnp.int32, (NBR, TILE), 1)
    high, low = halves(total)
    high, low = high.astype(F32), low.astype(F32)
    places, highs, lows = [], [], []
    for k in range(NBR):
        places.append(jnp.broadcast_to(place[k : k + 1], (16, TILE)).astype(jnp.int16))
        highs.append(jnp.broadcast_to(high[k : k + 1], (16, TILE)).astype(BF16))
        lows.append(jnp.broadcast_to(low[k : k + 1], (16, TILE)).astype(BF16))
    row = lax.broadcasted_iota(jnp.int16, (16, TILE), 0)
    for r in range(WINDOW // 16):
        here = row + jnp.int16(16 * r)
        a = jnp.zeros((16, TILE), BF16)
        b = jnp.zeros((16, TILE), BF16)
        for k in range(NBR):
            hit = places[k] == here
            a = jnp.where(hit, highs[k], a)
            b = jnp.where(hit, lows[k], b)
        high_ref[tile, 16 * r : 16 * r + 16, :] = a
        low_ref[tile, 16 * r : 16 * r + 16, :] = b


def two_tiles(ref, tile):
    blank = jnp.zeros((TILE, TILE), BF16)
    left = jnp.concatenate([ref[tile], blank], axis=0)
    right = jnp.concatenate([blank, ref[tile + 1]], axis=0)
    return jnp.concatenate([left, right], axis=1)


def kernel(
    fields,
    offsets,
    weights,
    vertical,
    source,
    share,
    count,
    target,
    new_fields,
    surface_flux,
    raw,
    near_offset,
    near_weight,
    mix_ref,
    mixed,
    mixed_halves,
    high_ref,
    low_ref,
    first,
    first_halves,
    second,
    outgoing,
    incoming,
    spread,
    flux,
    local_sem,
    send_sem,
    recv_sem,
    packet_send,
    packet_recv,
    out_sem,
):
    comp = lax.axis_index("comp")
    tile = lax.axis_index("tile")
    tiles = lax.axis_size("tile")
    column = comp // 2
    core = comp % 2
    is_ocean = column == OCEAN_X
    left = lax.rem(tile + tiles - 1, tiles)
    right = lax.rem(tile + 1, tiles)

    loads = [
        pltpu.make_async_copy(offsets, near_offset.at[:, pl.ds(HALO, CELLS)], local_sem.at[0]),
        pltpu.make_async_copy(weights, near_weight.at[:, pl.ds(HALO, CELLS)], local_sem.at[1]),
        pltpu.make_async_copy(fields, raw.at[:, pl.ds(2 * HALO, CELLS)], local_sem.at[2]),
    ]
    for load in loads:
        load.start()

    barrier = pltpu.get_barrier_semaphore()
    for side in (left, right):
        pl.semaphore_signal(barrier, inc=1, device_id=(comp, side), device_id_type=MESH)

    @pl.when(is_ocean)
    def _():
        for x in range(OCEAN_X):
            pl.semaphore_signal(barrier, inc=1, device_id=(2 * x + core, tile), device_id_type=MESH)
        pl.semaphore_wait(barrier, 2 + OCEAN_X)

    @pl.when(jnp.logical_not(is_ocean))
    def _():
        pl.semaphore_signal(
            barrier, inc=1, device_id=(2 * OCEAN_X + core, tile), device_id_type=MESH
        )
        pl.semaphore_wait(barrier, 3)

    def edges(ref, near, width, base):
        ahead = pltpu.make_async_remote_copy(
            src_ref=ref.at[:, pl.ds(CELLS - width, width)],
            dst_ref=near.at[:, pl.ds(0, width)],
            send_sem=send_sem.at[base],
            recv_sem=recv_sem.at[base],
            device_id=(comp, right),
            device_id_type=MESH,
        )
        back = pltpu.make_async_remote_copy(
            src_ref=ref.at[:, pl.ds(0, width)],
            dst_ref=near.at[:, pl.ds(width + CELLS, width)],
            send_sem=send_sem.at[base + 1],
            recv_sem=recv_sem.at[base + 1],
            device_id=(comp, left),
            device_id_type=MESH,
        )
        return [ahead, back]

    halo = edges(offsets, near_offset, HALO, 0)
    halo += edges(weights, near_weight, HALO, 2)
    halo += edges(fields, raw, 2 * HALO, 4)
    for copy in halo:
        copy.start()

    loads[0].wait()
    loads[1].wait()

    def build(t):
        build_tile(t, near_offset, near_weight, high_ref, low_ref)

    @pl.loop(0, CELLS // TILE)
    def _(t):
        build(t + HALO // TILE)

    own = vertical[0]
    rows = lax.broadcasted_iota(jnp.int32, (ROWS, ROWS), 0)
    columns = lax.broadcasted_iota(jnp.int32, (ROWS, ROWS), 1)
    unit = jnp.where(rows == columns, 1.0, 0.0).astype(F32)
    twice = unit + 2.0 * own + jnp.dot(own, own, precision=lax.Precision.HIGHEST)
    twice_high, twice_low = halves(twice)
    mix_ref[...] = jnp.concatenate(
        [twice_high.astype(F32), twice_high.astype(F32), twice_low.astype(F32)], axis=1
    ).astype(BF16)

    def mix(block):
        start = pl.multiple_of(block * BLOCK, BLOCK)
        high, low = halves(raw[:, pl.ds(start, BLOCK)])
        value = jnp.dot(
            mix_ref[...],
            jnp.concatenate([high, low, high], axis=0),
            preferred_element_type=F32,
        )
        mixed[:, pl.ds(start, BLOCK)] = value
        put_halves(mixed_halves, start, BLOCK, value)

    loads[2].wait()

    @pl.loop(0, CELLS // BLOCK)
    def _(block):
        mix(block + 2)

    for copy in halo:
        copy.wait()
    for t in (0, 1, NEAR // TILE - 2, NEAR // TILE - 1):
        build(t)
    for block in (0, 1, WIDE // BLOCK - 2, WIDE // BLOCK - 1):
        mix(block)

    def centre(start):
        return 1.0 - jnp.sum(near_weight[:, pl.ds(start, BLOCK)], axis=0, keepdims=True)

    @pl.loop(0, NEAR // BLOCK)
    def _(block):
        start = pl.multiple_of(block * BLOCK, BLOCK)
        window = mixed_halves[:, pl.ds(start, SPAN)]
        highs = jnp.concatenate([window[:SURF], window[2 * SURF : 2 * SURF + REST]], axis=0)
        by_high = jnp.dot(window, two_tiles(high_ref, 2 * block), preferred_element_type=F32)
        by_low = jnp.dot(highs, two_tiles(low_ref, 2 * block), preferred_element_type=F32)
        surf = by_high[:SURF] + by_high[SURF : 2 * SURF]
        rest = by_high[2 * SURF : 2 * SURF + REST] + by_high[2 * SURF + REST :]
        moved = jnp.concatenate([surf, rest], axis=0) + by_low
        here = mixed[:, pl.ds(pl.multiple_of(start + HALO, BLOCK), BLOCK)]
        value = centre(start) * here + moved
        first[:, pl.ds(start, BLOCK)] = value
        put_halves(first_halves, start, BLOCK, value)

    def second_update(block, row, height, half_row):
        start = pl.multiple_of(block * BLOCK, BLOCK)
        inner = pl.multiple_of(start + HALO, BLOCK)
        window = first_halves[half_row : half_row + 2 * height, pl.ds(start, SPAN)]
        by_high = jnp.dot(window, two_tiles(high_ref, 2 * block + 2), preferred_element_type=F32)
        by_low = jnp.dot(
            window[:height], two_tiles(low_ref, 2 * block + 2), preferred_element_type=F32
        )
        moved = by_high[:height] + by_high[height:] + by_low
        second[row : row + height, pl.ds(start, BLOCK)] = (
            centre(inner) * first[row : row + height, pl.ds(inner, BLOCK)] + moved
        )

    @pl.loop(0, CELLS // BLOCK)
    def _(block):
        second_update(block, 0, SURF, 0)

    packets = jnp.where(is_ocean, 3, 1)

    def packet_copy(i):
        row = jnp.where(is_ocean, i, 2 - column)
        to = jnp.where(is_ocean, row, OCEAN_X)
        slot = jnp.where(is_ocean, 0, row)
        return row, pltpu.make_async_remote_copy(
            src_ref=outgoing.at[i],
            dst_ref=incoming.at[slot],
            send_sem=packet_send.at[i],
            recv_sem=packet_recv.at[slot],
            device_id=(2 * to + core, tile),
            device_id_type=MESH,
        )

    @pl.loop(0, packets)
    def _(i):
        row, copy = packet_copy(i)
        live = count[0, row]

        @pl.loop(0, SLOTS // TILE)
        def _(p):
            start = pl.multiple_of(p * TILE, TILE)
            place = jnp.broadcast_to(row_of(source, row, pl.ds(start, TILE)), (8, TILE))
            lane = jnp.bitwise_and(place, TILE - 1)
            group = jnp.right_shift(place, 7)
            slot = start + lax.broadcasted_iota(jnp.int32, (8, TILE), 1)
            factor = jnp.where(
                slot < live,
                jnp.broadcast_to(row_of(share, row, pl.ds(start, TILE)), (8, TILE)),
                0.0,
            )
            parts = [jnp.zeros((8, TILE), F32) for _ in range(SURF // 8)]
            for g in range(CELLS // TILE):
                hit = group == g
                for s in range(SURF // 8):
                    block = second[8 * s : 8 * s + 8, g * TILE : g * TILE + TILE]
                    got = jnp.take_along_axis(block, lane, axis=1, mode="promise_in_bounds")
                    parts[s] = jnp.where(hit, got, parts[s])
            for s in range(SURF // 8):
                outgoing[i, 8 * s : 8 * s + 8, pl.ds(start, TILE)] = parts[s] * factor

        copy.start()

    @pl.loop(0, CELLS // BLOCK)
    def _(block):
        second_update(block, SURF, REST, 2 * SURF)

    store = pltpu.make_async_copy(second, new_fields, out_sem.at[0])
    store.start()

    @pl.loop(0, packets)
    def _(i):
        row = jnp.where(is_ocean, i, column)
        place = row_of(target, row, slice(None))
        lane = jnp.bitwise_and(place, TILE - 1)
        group = jnp.broadcast_to(jnp.right_shift(place, 7), (16, SLOTS)).astype(jnp.int16)
        lanes = lax.broadcasted_iota(jnp.int32, (TILE, SLOTS), 0)
        one_hot = jnp.where(lanes == lane, 1.0, 0.0).astype(BF16)
        pltpu.make_async_copy(incoming.at[i], incoming.at[i], packet_recv.at[i]).wait()
        high, low = halves(incoming[i])
        zero = jnp.zeros((SURF, SLOTS), BF16)
        for g in range(CELLS // TILE):
            hit = group == jnp.int16(g)
            spread[SURF * g : SURF * (g + 1), 0:SLOTS] = jnp.where(hit, high, zero)
            spread[SURF * g : SURF * (g + 1), SLOTS:] = jnp.where(hit, low, zero)
        landed = lax.dot_general(
            spread[...],
            jnp.concatenate([one_hot, one_hot], axis=1),
            (((1,), (1,)), ((), ())),
            preferred_element_type=F32,
        )

        @pl.when(i == 0)
        def _():
            for g in range(CELLS // TILE):
                flux[:, g * TILE : (g + 1) * TILE] = landed[SURF * g : SURF * (g + 1)]

        @pl.when(i > 0)
        def _():
            for g in range(CELLS // TILE):
                flux[:, g * TILE : (g + 1) * TILE] += landed[SURF * g : SURF * (g + 1)]

    last = pltpu.make_async_copy(flux, surface_flux, out_sem.at[1])
    last.start()

    @pl.loop(0, packets)
    def _(i):
        pltpu.make_async_copy(outgoing.at[i], outgoing.at[i], packet_send.at[i]).wait()

    store.wait()
    last.wait()


def local(*args):
    hbm = pl.BlockSpec(memory_space=pl.ANY)
    vmem = pl.BlockSpec(memory_space=pltpu.VMEM)
    smem = pl.BlockSpec(memory_space=pltpu.SMEM)
    return pl.pallas_call(
        kernel,
        out_shape=(
            jax.ShapeDtypeStruct((ROWS, CELLS), F32),
            jax.ShapeDtypeStruct((SURF, CELLS), F32),
        ),
        in_specs=[hbm, hbm, hbm, vmem, vmem, vmem, smem, vmem],
        out_specs=(hbm, hbm),
        scratch_shapes=[
            pltpu.VMEM((ROWS, WIDE), F32),
            pltpu.VMEM((NBR, NEAR), jnp.int32),
            pltpu.VMEM((NBR, NEAR), F32),
            pltpu.VMEM((ROWS, 3 * ROWS), BF16),
            pltpu.VMEM((ROWS, WIDE), F32),
            pltpu.VMEM((2 * ROWS, WIDE), BF16),
            pltpu.VMEM((NEAR // TILE, WINDOW, TILE), BF16),
            pltpu.VMEM((NEAR // TILE, WINDOW, TILE), BF16),
            pltpu.VMEM((ROWS, NEAR), F32),
            pltpu.VMEM((2 * ROWS, NEAR), BF16),
            pltpu.VMEM((ROWS, CELLS), F32),
            pltpu.VMEM((3, SURF, SLOTS), F32),
            pltpu.VMEM((3, SURF, SLOTS), F32),
            pltpu.VMEM((SURF * CELLS // TILE, 2 * SLOTS), BF16),
            pltpu.VMEM((SURF, CELLS), F32),
            pltpu.SemaphoreType.DMA((3,)),
            pltpu.SemaphoreType.DMA((6,)),
            pltpu.SemaphoreType.DMA((6,)),
            pltpu.SemaphoreType.DMA((3,)),
            pltpu.SemaphoreType.DMA((3,)),
            pltpu.SemaphoreType.DMA((2,)),
        ],
        compiler_params=pltpu.CompilerParams(
            collective_id=0, has_side_effects=True, vmem_limit_bytes=40 << 20
        ),
        name="coupled_update",
    )(*args)


def solution(mesh):
    placed = (
        P(None, ("comp", "tile")),
        P(None, ("comp", "tile")),
        P(None, ("comp", "tile")),
        P("comp", None, None),
        P(("comp", "tile"), None),
        P(("comp", "tile"), None),
        P(("comp", "tile"), None),
        P(("comp", "tile"), None),
    )
    return jax.shard_map(
        local,
        mesh=mesh,
        in_specs=placed,
        out_specs=(P(None, ("comp", "tile")), P(None, ("comp", "tile"))),
        check_vma=False,
    )
```

```python
import jax
import jax.numpy as jnp
from jax import lax
from jax.experimental import pallas as pl
from jax.experimental.pallas import tpu as pltpu
from jax.sharding import PartitionSpec as P

ROWS = 80
SURF = 16
REST = ROWS - SURF
NBR = 8
CELLS = 4096
HALO = 256
SLOTS = 1024
TILE = 128
BLOCK = 256
WINDOW = TILE + 2 * HALO
SPAN = BLOCK + 2 * HALO
NEAR = CELLS + 2 * HALO
WIDE = CELLS + 4 * HALO
HALF = SLOTS // 2
OCEAN_X = 3
BF16 = jnp.bfloat16
F32 = jnp.float32
MESH = pl.DeviceIdType.MESH


def halves(value):
    high = value.astype(BF16)
    return high, (value - high.astype(F32)).astype(BF16)


def put_halves(ref, column, width, value):
    high, low = halves(value)
    columns = pl.ds(column, width)
    ref[0:SURF, columns] = high[:SURF]
    ref[SURF : 2 * SURF, columns] = low[:SURF]
    ref[2 * SURF : 2 * SURF + REST, columns] = high[SURF:]
    ref[2 * SURF + REST :, columns] = low[SURF:]


def row_of(ref, row, columns):
    second_or_third = jnp.where(row == 1, ref[1:2, columns], ref[2:3, columns])
    return jnp.where(row == 0, ref[0:1, columns], second_or_third)


def build_block(block, offset_ref, weight_ref, high_ref, low_ref, slot):
    for side in range(2):
        columns = pl.ds(pl.multiple_of(block * BLOCK + side * TILE, TILE), TILE)
        offset = offset_ref[:, columns]
        weight = weight_ref[:, columns]
        total = weight
        for shift in range(1, NBR):
            same = pltpu.roll(offset, shift, 0) == offset
            total = total + jnp.where(same, pltpu.roll(weight, shift, 0), 0.0)
        place = offset + HALO + lax.broadcasted_iota(jnp.int32, (NBR, TILE), 1)
        high, low = halves(total)
        high, low = high.astype(F32), low.astype(F32)
        places, highs, lows = [], [], []
        for k in range(NBR):
            places.append(jnp.broadcast_to(place[k : k + 1], (16, TILE)).astype(jnp.int16))
            highs.append(jnp.broadcast_to(high[k : k + 1], (16, TILE)).astype(BF16))
            lows.append(jnp.broadcast_to(low[k : k + 1], (16, TILE)).astype(BF16))
        row = lax.broadcasted_iota(jnp.int16, (16, TILE), 0)
        for r in range(WINDOW // 16):
            here = row + jnp.int16(16 * r)
            a = jnp.zeros((16, TILE), BF16)
            b = jnp.zeros((16, TILE), BF16)
            for k in range(NBR):
                hit = places[k] == here
                a = jnp.where(hit, highs[k], a)
                b = jnp.where(hit, lows[k], b)
            high_ref[slot, side, 16 * r : 16 * r + 16, :] = a
            low_ref[slot, side, 16 * r : 16 * r + 16, :] = b


def matrix(ref, slot):
    blank = jnp.zeros((TILE, TILE), BF16)
    left = jnp.concatenate([ref[slot, 0], blank], axis=0)
    right = jnp.concatenate([blank, ref[slot, 1]], axis=0)
    return jnp.concatenate([left, right], axis=1)


def kernel(
    fields,
    offsets,
    weights,
    vertical_in,
    source_in,
    share_in,
    count_in,
    target_in,
    second,
    flux,
    raw,
    near_offset,
    near_weight,
    mix_ref,
    mixed,
    mixed_halves,
    even_high,
    even_low,
    odd_high,
    odd_low,
    first,
    first_halves,
    outgoing,
    incoming,
    spread,
    vertical,
    source,
    share,
    target,
    count,
    local_sem,
    send_sem,
    recv_sem,
    packet_send,
    packet_recv,
):
    comp = lax.axis_index("comp")
    tile = lax.axis_index("tile")
    tiles = lax.axis_size("tile")
    column = comp // 2
    core = comp % 2
    is_ocean = column == OCEAN_X
    left = lax.rem(tile + tiles - 1, tiles)
    right = lax.rem(tile + 1, tiles)

    loads = []
    for ref, place in (
        (offsets, near_offset.at[:, pl.ds(HALO, CELLS)]),
        (weights, near_weight.at[:, pl.ds(HALO, CELLS)]),
        (vertical_in, vertical),
        (fields, raw.at[:, pl.ds(2 * HALO, CELLS)]),
        (source_in, source),
        (share_in, share),
        (count_in, count),
        (target_in, target),
    ):
        loads.append(pltpu.make_async_copy(ref, place, local_sem.at[len(loads)]))
        loads[-1].start()

    barrier = pltpu.get_barrier_semaphore()
    for side in (left, right):
        pl.semaphore_signal(barrier, inc=1, device_id=(comp, side), device_id_type=MESH)

    @pl.when(is_ocean)
    def _():
        for x in range(OCEAN_X):
            pl.semaphore_signal(barrier, inc=1, device_id=(2 * x + core, tile), device_id_type=MESH)

    @pl.when(jnp.logical_not(is_ocean))
    def _():
        pl.semaphore_signal(
            barrier, inc=1, device_id=(2 * OCEAN_X + core, tile), device_id_type=MESH
        )

    def edges(ref, near, width, base):
        ahead = pltpu.make_async_remote_copy(
            src_ref=ref.at[:, pl.ds(CELLS - width, width)],
            dst_ref=near.at[:, pl.ds(0, width)],
            send_sem=send_sem.at[base],
            recv_sem=recv_sem.at[base],
            device_id=(comp, right),
            device_id_type=MESH,
        )
        back = pltpu.make_async_remote_copy(
            src_ref=ref.at[:, pl.ds(0, width)],
            dst_ref=near.at[:, pl.ds(width + CELLS, width)],
            send_sem=send_sem.at[base + 1],
            recv_sem=recv_sem.at[base + 1],
            device_id=(comp, left),
            device_id_type=MESH,
        )
        return [ahead, back]

    halo = edges(offsets, near_offset, HALO, 0)
    halo += edges(weights, near_weight, HALO, 2)
    halo += edges(fields, raw, 2 * HALO, 4)
    loads[0].wait()
    loads[1].wait()

    highs_by = (even_high, odd_high)
    lows_by = (even_low, odd_low)

    def build(block, parity, slot):
        build_block(
            block, near_offset, near_weight, highs_by[parity], lows_by[parity], slot
        )

    build(1, 1, 0)
    build(2, 0, 1)
    loads[2].wait()

    own = vertical[0]
    rows = lax.broadcasted_iota(jnp.int32, (ROWS, ROWS), 0)
    columns = lax.broadcasted_iota(jnp.int32, (ROWS, ROWS), 1)
    unit = jnp.where(rows == columns, 1.0, 0.0).astype(F32)
    twice = unit + 2.0 * own + jnp.dot(own, own, precision=lax.Precision.HIGHEST)
    twice_high, twice_low = halves(twice)
    mix_ref[...] = jnp.concatenate(
        [twice_high.astype(F32), twice_high.astype(F32), twice_low.astype(F32)], axis=1
    ).astype(BF16)

    def mix(block):
        start = pl.multiple_of(block * BLOCK, BLOCK)
        high, low = halves(raw[:, pl.ds(start, BLOCK)])
        value = jnp.dot(
            mix_ref[...],
            jnp.concatenate([high, low, high], axis=0),
            preferred_element_type=F32,
        )
        mixed[:, pl.ds(start, BLOCK)] = value
        put_halves(mixed_halves, start, BLOCK, value)

    def centre(start):
        return 1.0 - jnp.sum(near_weight[:, pl.ds(start, BLOCK)], axis=0, keepdims=True)

    def first_update(block, parity, slot):
        start = pl.multiple_of(block * BLOCK, BLOCK)
        window = mixed_halves[:, pl.ds(start, SPAN)]
        highs = jnp.concatenate([window[:SURF], window[2 * SURF : 2 * SURF + REST]], axis=0)
        by_high = jnp.dot(window, matrix(highs_by[parity], slot), preferred_element_type=F32)
        by_low = jnp.dot(highs, matrix(lows_by[parity], slot), preferred_element_type=F32)
        surf = by_high[:SURF] + by_high[SURF : 2 * SURF]
        rest = by_high[2 * SURF : 2 * SURF + REST] + by_high[2 * SURF + REST :]
        moved = jnp.concatenate([surf, rest], axis=0) + by_low
        here = mixed[:, pl.ds(pl.multiple_of(start + HALO, BLOCK), BLOCK)]
        value = centre(start) * here + moved
        first[:, pl.ds(start, BLOCK)] = value
        put_halves(first_halves, start, BLOCK, value)

    loads[3].wait()
    for block in (2, 3, 4):
        mix(block)

    def second_update(pair, parity, row, height, half_row):
        start = pl.multiple_of((2 * pair + parity) * BLOCK, BLOCK)
        inner = pl.multiple_of(start + HALO, BLOCK)
        window = first_halves[half_row : half_row + 2 * height, pl.ds(start, SPAN)]
        slot = pair + parity
        by_high = jnp.dot(
            window, matrix(highs_by[1 - parity], slot), preferred_element_type=F32
        )
        by_low = jnp.dot(
            window[:height], matrix(lows_by[1 - parity], slot), preferred_element_type=F32
        )
        moved = by_high[:height] + by_high[height:] + by_low
        second[row : row + height, pl.ds(start, BLOCK)] = (
            centre(inner) * first[row : row + height, pl.ds(inner, BLOCK)] + moved
        )

    last = CELLS // BLOCK

    def fused(pairs, with_surface):
        @pl.loop(*pairs)
        def _(pair):
            for parity in range(2):
                block = 2 * pair + parity
                first_update(block, parity, pair)
                if with_surface:
                    second_update(pair - 2 + parity, 1 - parity, 0, SURF, 0)
                build(block + 1, 1 - parity, pair + parity)
                mix(block + 3)

    def surface(block):
        second_update(block // 2, block % 2, 0, SURF, 0)

    @pl.when(is_ocean)
    def _():
        pl.semaphore_wait(barrier, 2 + OCEAN_X)

    @pl.when(jnp.logical_not(is_ocean))
    def _():
        pl.semaphore_wait(barrier, 3)

    for copy in halo:
        copy.start()
    fused((1, 3), False)
    fused((3, last // 2 - 1), True)
    first_update(last - 2, 0, last // 2 - 1)
    surface(last - 5)
    build(last - 1, 1, last // 2 - 1)
    mix(last + 1)
    first_update(last - 1, 1, last // 2 - 1)
    surface(last - 4)
    build(last, 0, last // 2)
    for copy in halo:
        copy.wait()
    for block in (last + 2, last + 3, 0, 1):
        mix(block)
    first_update(last, 0, last // 2)
    surface(last - 3)
    build(last + 1, 1, last // 2)
    first_update(last + 1, 1, last // 2)
    surface(last - 2)
    build(0, 0, 0)
    surface(last - 1)
    first_update(0, 0, 0)
    first_update(1, 1, 0)
    for block in range(3):
        surface(block)

    for load in loads[4:]:
        load.wait()

    packets = jnp.where(is_ocean, 3, 1)

    def packet_copies(i):
        row = jnp.where(is_ocean, jnp.where(i == 2, 2, 1 - i), 2 - column)
        to = jnp.where(is_ocean, row, OCEAN_X)
        slot = jnp.where(is_ocean, 0, row)
        return row, [
            pltpu.make_async_remote_copy(
                src_ref=outgoing.at[i, :, pl.ds(half * HALF, HALF)],
                dst_ref=incoming.at[slot, :, pl.ds(half * HALF, HALF)],
                send_sem=packet_send.at[i, half],
                recv_sem=packet_recv.at[slot, half],
                device_id=(2 * to + core, tile),
                device_id_type=MESH,
            )
            for half in range(2)
        ]

    @pl.loop(0, packets)
    def _(i):
        row, copies = packet_copies(i)
        live = count[0, row]
        for half, copy in enumerate(copies):

            @pl.loop(half * HALF // TILE, (half + 1) * HALF // TILE)
            def _(p):
                start = pl.multiple_of(p * TILE, TILE)
                place = jnp.broadcast_to(row_of(source, row, pl.ds(start, TILE)), (8, TILE))
                lane = jnp.bitwise_and(place, TILE - 1)
                group = jnp.right_shift(place, 7)
                slot = start + lax.broadcasted_iota(jnp.int32, (8, TILE), 1)
                factor = jnp.where(
                    slot < live,
                    jnp.broadcast_to(row_of(share, row, pl.ds(start, TILE)), (8, TILE)),
                    0.0,
                )
                parts = [jnp.zeros((8, TILE), F32) for _ in range(SURF // 8)]
                for g in range(CELLS // TILE):
                    hit = group == g
                    for s in range(SURF // 8):
                        block = second[8 * s : 8 * s + 8, g * TILE : g * TILE + TILE]
                        got = jnp.take_along_axis(block, lane, axis=1, mode="promise_in_bounds")
                        parts[s] = jnp.where(hit, got, parts[s])
                for s in range(SURF // 8):
                    outgoing[i, 8 * s : 8 * s + 8, pl.ds(start, TILE)] = parts[s] * factor

            copy.start()

    @pl.loop(0, last // 2)
    def _(pair):
        for parity in range(2):
            second_update(pair, parity, SURF, REST, 2 * SURF)

    @pl.loop(0, packets)
    def _(i):
        slot = jnp.where(is_ocean, jnp.where(i == 0, 0, 3 - i), 0)
        row = jnp.where(is_ocean, slot, column)
        place = row_of(target, row, slice(None))
        lane = jnp.bitwise_and(place, TILE - 1)
        group = jnp.broadcast_to(jnp.right_shift(place, 7), (16, SLOTS)).astype(jnp.int16)
        lanes = lax.broadcasted_iota(jnp.int32, (TILE, SLOTS), 0)
        one_hot = jnp.where(lanes == lane, 1.0, 0.0).astype(BF16)
        for half in range(2):
            part = incoming.at[slot, :, pl.ds(half * HALF, HALF)]
            pltpu.make_async_copy(part, part, packet_recv.at[slot, half]).wait()
        high, low = halves(incoming[slot])
        zero = jnp.zeros((SURF, SLOTS), BF16)
        for g in range(CELLS // TILE):
            hit = group == jnp.int16(g)
            spread[SURF * g : SURF * (g + 1), 0:SLOTS] = jnp.where(hit, high, zero)
            spread[SURF * g : SURF * (g + 1), SLOTS:] = jnp.where(hit, low, zero)
        landed = lax.dot_general(
            spread[...],
            jnp.concatenate([one_hot, one_hot], axis=1),
            (((1,), (1,)), ((), ())),
            preferred_element_type=F32,
        )

        @pl.when(i == 0)
        def _():
            for g in range(CELLS // TILE):
                flux[:, g * TILE : (g + 1) * TILE] = landed[SURF * g : SURF * (g + 1)]

        @pl.when(i > 0)
        def _():
            for g in range(CELLS // TILE):
                flux[:, g * TILE : (g + 1) * TILE] += landed[SURF * g : SURF * (g + 1)]

    @pl.loop(0, packets)
    def _(i):
        for half in range(2):
            part = outgoing.at[i, :, pl.ds(half * HALF, HALF)]
            pltpu.make_async_copy(part, part, packet_send.at[i, half]).wait()


def local(*args):
    hbm = pl.BlockSpec(memory_space=pltpu.HBM)
    vmem = pl.BlockSpec(memory_space=pltpu.VMEM)
    return pl.pallas_call(
        kernel,
        out_shape=(
            pltpu.VMEM((ROWS, CELLS), F32),
            pltpu.VMEM((SURF, CELLS), F32),
        ),
        in_specs=[hbm] * 8,
        out_specs=(vmem, vmem),
        scratch_shapes=[
            pltpu.VMEM((ROWS, WIDE), F32),
            pltpu.VMEM((NBR, NEAR), jnp.int32),
            pltpu.VMEM((NBR, NEAR), F32),
            pltpu.VMEM((ROWS, 3 * ROWS), BF16),
            pltpu.VMEM((ROWS, WIDE), F32),
            pltpu.VMEM((2 * ROWS, WIDE), BF16),
            pltpu.VMEM((NEAR // BLOCK // 2, 2, WINDOW, TILE), BF16),
            pltpu.VMEM((NEAR // BLOCK // 2, 2, WINDOW, TILE), BF16),
            pltpu.VMEM((NEAR // BLOCK // 2, 2, WINDOW, TILE), BF16),
            pltpu.VMEM((NEAR // BLOCK // 2, 2, WINDOW, TILE), BF16),
            pltpu.VMEM((ROWS, NEAR), F32),
            pltpu.VMEM((2 * ROWS, NEAR), BF16),
            pltpu.VMEM((3, SURF, SLOTS), F32),
            pltpu.VMEM((3, SURF, SLOTS), F32),
            pltpu.VMEM((SURF * CELLS // TILE, 2 * SLOTS), BF16),
            pltpu.VMEM((1, ROWS, ROWS), F32),
            pltpu.VMEM((3, SLOTS), jnp.int32),
            pltpu.VMEM((3, SLOTS), F32),
            pltpu.VMEM((3, SLOTS), jnp.int32),
            pltpu.SMEM((1, 3), jnp.int32),
            pltpu.SemaphoreType.DMA((8,)),
            pltpu.SemaphoreType.DMA((6,)),
            pltpu.SemaphoreType.DMA((6,)),
            pltpu.SemaphoreType.DMA((3, 2)),
            pltpu.SemaphoreType.DMA((3, 2)),
        ],
        compiler_params=pltpu.CompilerParams(
            collective_id=0, has_side_effects=True, vmem_limit_bytes=124 << 19
        ),
        name="coupled_update",
    )(*args)


def solution(mesh):
    placed = (
        P(None, ("comp", "tile")),
        P(None, ("comp", "tile")),
        P(None, ("comp", "tile")),
        P("comp", None, None),
        P(("comp", "tile"), None),
        P(("comp", "tile"), None),
        P(("comp", "tile"), None),
        P(("comp", "tile"), None),
    )
    return jax.shard_map(
        local,
        mesh=mesh,
        in_specs=placed,
        out_specs=(P(None, ("comp", "tile")), P(None, ("comp", "tile"))),
        check_vma=False,
    )
```

```python
import jax
import jax.numpy as jnp
from jax import lax
from jax.experimental import pallas as pl
from jax.experimental.pallas import tpu as pltpu
from jax.sharding import PartitionSpec as P

ROWS = 80
SURF = 16
REST = ROWS - SURF
NBR = 8
CELLS = 4096
HALO = 256
SLOTS = 1024
TILE = 128
BLOCK = 256
WINDOW = TILE + 2 * HALO
SPAN = BLOCK + 2 * HALO
NEAR = CELLS + 2 * HALO
WIDE = CELLS + 4 * HALO
HALF = SLOTS // 2
OCEAN_X = 3
BF16 = jnp.bfloat16
F32 = jnp.float32
MESH = pl.DeviceIdType.MESH


def halves(value):
    high = value.astype(BF16)
    return high, (value - high.astype(F32)).astype(BF16)


def put_halves(ref, column, width, value):
    high, low = halves(value)
    columns = pl.ds(column, width)
    ref[0:SURF, columns] = high[:SURF]
    ref[SURF : 2 * SURF, columns] = low[:SURF]
    ref[2 * SURF : 2 * SURF + REST, columns] = high[SURF:]
    ref[2 * SURF + REST :, columns] = low[SURF:]


def row_of(ref, row, columns):
    second_or_third = jnp.where(row == 1, ref[1:2, columns], ref[2:3, columns])
    return jnp.where(row == 0, ref[0:1, columns], second_or_third)


def build_block(block, offset_ref, weight_ref, high_ref, low_ref, slot):
    for side in range(2):
        columns = pl.ds(pl.multiple_of(block * BLOCK + side * TILE, TILE), TILE)
        offset = offset_ref[:, columns]
        weight = weight_ref[:, columns]
        total = weight
        for shift in range(1, NBR):
            same = pltpu.roll(offset, shift, 0) == offset
            total = total + jnp.where(same, pltpu.roll(weight, shift, 0), 0.0)
        place = offset + HALO + lax.broadcasted_iota(jnp.int32, (NBR, TILE), 1)
        high, low = halves(total)
        high, low = high.astype(F32), low.astype(F32)
        places, highs, lows = [], [], []
        for k in range(NBR):
            places.append(jnp.broadcast_to(place[k : k + 1], (16, TILE)).astype(jnp.int16))
            highs.append(jnp.broadcast_to(high[k : k + 1], (16, TILE)).astype(BF16))
            lows.append(jnp.broadcast_to(low[k : k + 1], (16, TILE)).astype(BF16))
        row = lax.broadcasted_iota(jnp.int16, (16, TILE), 0)
        for r in range(WINDOW // 16):
            here = row + jnp.int16(16 * r)
            a = jnp.zeros((16, TILE), BF16)
            b = jnp.zeros((16, TILE), BF16)
            for k in range(NBR):
                hit = places[k] == here
                a = jnp.where(hit, highs[k], a)
                b = jnp.where(hit, lows[k], b)
            high_ref[slot, side, 16 * r : 16 * r + 16, :] = a
            low_ref[slot, side, 16 * r : 16 * r + 16, :] = b


def matrix(ref, slot):
    blank = jnp.zeros((TILE, TILE), BF16)
    left = jnp.concatenate([ref[slot, 0], blank], axis=0)
    right = jnp.concatenate([blank, ref[slot, 1]], axis=0)
    return jnp.concatenate([left, right], axis=1)


def kernel(
    fields,
    offsets,
    weights,
    vertical_in,
    source_in,
    share_in,
    count_in,
    target_in,
    second,
    incoming,
    target,
    raw,
    near_offset,
    near_weight,
    mix_ref,
    mixed,
    mixed_halves,
    even_high,
    even_low,
    odd_high,
    odd_low,
    first,
    first_halves,
    outgoing,
    surface_halves,
    vertical,
    source,
    share,
    count,
    local_sem,
    send_sem,
    recv_sem,
    packet_send,
    packet_recv,
):
    comp = lax.axis_index("comp")
    tile = lax.axis_index("tile")
    tiles = lax.axis_size("tile")
    column = comp // 2
    core = comp % 2
    is_ocean = column == OCEAN_X
    left = lax.rem(tile + tiles - 1, tiles)
    right = lax.rem(tile + 1, tiles)

    loads = []
    for ref, place in (
        (offsets, near_offset.at[:, pl.ds(HALO, CELLS)]),
        (weights, near_weight.at[:, pl.ds(HALO, CELLS)]),
        (vertical_in, vertical),
        (fields, raw.at[:, pl.ds(2 * HALO, CELLS)]),
        (source_in, source),
        (share_in, share),
        (count_in, count),
        (target_in, target),
    ):
        loads.append(pltpu.make_async_copy(ref, place, local_sem.at[len(loads)]))
        loads[-1].start()

    barrier = pltpu.get_barrier_semaphore()
    for side in (left, right):
        pl.semaphore_signal(barrier, inc=1, device_id=(comp, side), device_id_type=MESH)

    @pl.when(is_ocean)
    def _():
        for x in range(OCEAN_X):
            pl.semaphore_signal(barrier, inc=1, device_id=(2 * x + core, tile), device_id_type=MESH)

    @pl.when(jnp.logical_not(is_ocean))
    def _():
        pl.semaphore_signal(
            barrier, inc=1, device_id=(2 * OCEAN_X + core, tile), device_id_type=MESH
        )

    def edges(ref, near, width, base):
        ahead = pltpu.make_async_remote_copy(
            src_ref=ref.at[:, pl.ds(CELLS - width, width)],
            dst_ref=near.at[:, pl.ds(0, width)],
            send_sem=send_sem.at[base],
            recv_sem=recv_sem.at[base],
            device_id=(comp, right),
            device_id_type=MESH,
        )
        back = pltpu.make_async_remote_copy(
            src_ref=ref.at[:, pl.ds(0, width)],
            dst_ref=near.at[:, pl.ds(width + CELLS, width)],
            send_sem=send_sem.at[base + 1],
            recv_sem=recv_sem.at[base + 1],
            device_id=(comp, left),
            device_id_type=MESH,
        )
        return [ahead, back]

    halo = edges(fields, raw, 2 * HALO, 4)
    halo += edges(offsets, near_offset, HALO, 0)
    halo += edges(weights, near_weight, HALO, 2)
    loads[0].wait()
    loads[1].wait()

    highs_by = (even_high, odd_high)
    lows_by = (even_low, odd_low)

    def build(block, parity, slot):
        build_block(
            block, near_offset, near_weight, highs_by[parity], lows_by[parity], slot
        )

    build(1, 1, 0)
    build(2, 0, 1)
    loads[2].wait()

    own = vertical[0]
    rows = lax.broadcasted_iota(jnp.int32, (ROWS, ROWS), 0)
    columns = lax.broadcasted_iota(jnp.int32, (ROWS, ROWS), 1)
    unit = jnp.where(rows == columns, 1.0, 0.0).astype(F32)
    twice = unit + 2.0 * own + jnp.dot(own, own, precision=lax.Precision.HIGHEST)
    twice_high, twice_low = halves(twice)
    mix_ref[...] = jnp.concatenate(
        [twice_high.astype(F32), twice_high.astype(F32), twice_low.astype(F32)], axis=1
    ).astype(BF16)

    def mix(block):
        start = pl.multiple_of(block * BLOCK, BLOCK)
        high, low = halves(raw[:, pl.ds(start, BLOCK)])
        value = jnp.dot(
            mix_ref[...],
            jnp.concatenate([high, low, high], axis=0),
            preferred_element_type=F32,
        )
        mixed[:, pl.ds(start, BLOCK)] = value
        put_halves(mixed_halves, start, BLOCK, value)

    def centre(start):
        return 1.0 - jnp.sum(near_weight[:, pl.ds(start, BLOCK)], axis=0, keepdims=True)

    def first_update(block, parity, slot):
        start = pl.multiple_of(block * BLOCK, BLOCK)
        window = mixed_halves[:, pl.ds(start, SPAN)]
        highs = jnp.concatenate([window[:SURF], window[2 * SURF : 2 * SURF + REST]], axis=0)
        by_high = jnp.dot(window, matrix(highs_by[parity], slot), preferred_element_type=F32)
        by_low = jnp.dot(highs, matrix(lows_by[parity], slot), preferred_element_type=F32)
        surf = by_high[:SURF] + by_high[SURF : 2 * SURF]
        rest = by_high[2 * SURF : 2 * SURF + REST] + by_high[2 * SURF + REST :]
        moved = jnp.concatenate([surf, rest], axis=0) + by_low
        here = mixed[:, pl.ds(pl.multiple_of(start + HALO, BLOCK), BLOCK)]
        value = centre(start) * here + moved
        first[:, pl.ds(start, BLOCK)] = value
        put_halves(first_halves, start, BLOCK, value)

    loads[3].wait()
    for block in (2, 3, 4):
        mix(block)

    def second_update(pair, parity, row, height, half_row):
        start = pl.multiple_of((2 * pair + parity) * BLOCK, BLOCK)
        inner = pl.multiple_of(start + HALO, BLOCK)
        window = first_halves[half_row : half_row + 2 * height, pl.ds(start, SPAN)]
        slot = pair + parity
        by_high = jnp.dot(
            window, matrix(highs_by[1 - parity], slot), preferred_element_type=F32
        )
        by_low = jnp.dot(
            window[:height], matrix(lows_by[1 - parity], slot), preferred_element_type=F32
        )
        moved = by_high[:height] + by_high[height:] + by_low
        second[row : row + height, pl.ds(start, BLOCK)] = (
            centre(inner) * first[row : row + height, pl.ds(inner, BLOCK)] + moved
        )

    last = CELLS // BLOCK

    def fused(pairs, with_surface):
        @pl.loop(*pairs)
        def _(pair):
            for parity in range(2):
                block = 2 * pair + parity
                first_update(block, parity, pair)
                if with_surface:
                    second_update(pair - 2 + parity, 1 - parity, 0, SURF, 0)
                build(block + 1, 1 - parity, pair + parity)
                mix(block + 3)

    def surface(block):
        second_update(block // 2, block % 2, 0, SURF, 0)

    @pl.when(is_ocean)
    def _():
        pl.semaphore_wait(barrier, 2 + OCEAN_X)

    @pl.when(jnp.logical_not(is_ocean))
    def _():
        pl.semaphore_wait(barrier, 3)

    for copy in halo:
        copy.start()
    fused((1, 3), False)
    fused((3, last // 2 - 1), True)
    first_update(last - 2, 0, last // 2 - 1)
    surface(last - 5)
    build(last - 1, 1, last // 2 - 1)
    mix(last + 1)
    first_update(last - 1, 1, last // 2 - 1)
    surface(last - 4)
    build(last, 0, last // 2)
    for copy in halo:
        copy.wait()
    for block in (last + 2, last + 3, 0, 1):
        mix(block)
    first_update(last, 0, last // 2)
    surface(last - 3)
    build(last + 1, 1, last // 2)
    first_update(last + 1, 1, last // 2)
    surface(last - 2)
    build(0, 0, 0)
    surface(last - 1)
    first_update(0, 0, 0)
    first_update(1, 1, 0)
    for block in range(3):
        surface(block)

    for g in range(CELLS // TILE):
        high, low = halves(second[0:SURF, g * TILE : (g + 1) * TILE])
        surface_halves[SURF * g : SURF * (g + 1), 0:TILE] = high
        surface_halves[SURF * g : SURF * (g + 1), TILE:] = low

    for load in loads[4:]:
        load.wait()

    packets = jnp.where(is_ocean, 3, 1)

    def packet_copies(i):
        row = jnp.where(is_ocean, jnp.where(i == 2, 2, 1 - i), 2 - column)
        to = jnp.where(is_ocean, row, OCEAN_X)
        slot = jnp.where(is_ocean, 0, row)
        return row, [
            pltpu.make_async_remote_copy(
                src_ref=outgoing.at[i, :, pl.ds(half * HALF, HALF)],
                dst_ref=incoming.at[slot, :, pl.ds(half * HALF, HALF)],
                send_sem=packet_send.at[i, half],
                recv_sem=packet_recv.at[slot, half],
                device_id=(2 * to + core, tile),
                device_id_type=MESH,
            )
            for half in range(2)
        ]

    @pl.loop(0, packets)
    def _(i):
        row, copies = packet_copies(i)
        live = count[0, row]
        for half, copy in enumerate(copies):

            @pl.loop(half * HALF // BLOCK, (half + 1) * HALF // BLOCK)
            def _(p):
                start = pl.multiple_of(p * BLOCK, BLOCK)
                columns = pl.ds(start, BLOCK)
                place = row_of(source, row, columns)
                lane = jnp.bitwise_and(place, TILE - 1)
                lanes = lax.broadcasted_iota(jnp.int32, (TILE, BLOCK), 0)
                one_hot = jnp.where(lanes == lane, 1.0, 0.0).astype(BF16)
                got = jnp.dot(
                    surface_halves[...],
                    jnp.concatenate([one_hot, one_hot], axis=0),
                    preferred_element_type=F32,
                )
                group = jnp.broadcast_to(jnp.right_shift(place, 7), (SURF, BLOCK))
                slot = start + lax.broadcasted_iota(jnp.int32, (SURF, BLOCK), 1)
                factor = jnp.where(slot < live, row_of(share, row, columns), 0.0)
                picked = jnp.zeros((SURF, BLOCK), F32)
                for g in range(CELLS // TILE):
                    picked = jnp.where(group == g, got[SURF * g : SURF * (g + 1)], picked)
                outgoing[i, :, columns] = picked * factor

            copy.start()

    @pl.loop(0, last // 2)
    def _(pair):
        for parity in range(2):
            second_update(pair, parity, SURF, REST, 2 * SURF)

    @pl.loop(0, packets)
    def _(i):
        for half in range(2):
            part = incoming.at[i, :, pl.ds(half * HALF, HALF)]
            pltpu.make_async_copy(part, part, packet_recv.at[i, half]).wait()
            part = outgoing.at[i, :, pl.ds(half * HALF, HALF)]
            pltpu.make_async_copy(part, part, packet_send.at[i, half]).wait()


def landing(second, incoming, target, new_fields, surface_flux, spread, flux, store_sem):
    comp = lax.axis_index("comp")
    column = comp // 2
    is_ocean = column == OCEAN_X
    store = pltpu.make_async_copy(second, new_fields, store_sem.at[0])
    store.start()

    @pl.loop(0, jnp.where(is_ocean, 3, 1))
    def _(i):
        row = jnp.where(is_ocean, i, column)
        place = row_of(target, row, slice(None))
        lane = jnp.bitwise_and(place, TILE - 1)
        group = jnp.broadcast_to(jnp.right_shift(place, 7), (16, SLOTS)).astype(jnp.int16)
        lanes = lax.broadcasted_iota(jnp.int32, (TILE, SLOTS), 0)
        one_hot = jnp.where(lanes == lane, 1.0, 0.0).astype(BF16)
        high, low = halves(incoming[i])
        zero = jnp.zeros((SURF, SLOTS), BF16)
        for g in range(CELLS // TILE):
            hit = group == jnp.int16(g)
            spread[SURF * g : SURF * (g + 1), 0:SLOTS] = jnp.where(hit, high, zero)
            spread[SURF * g : SURF * (g + 1), SLOTS:] = jnp.where(hit, low, zero)
        landed = lax.dot_general(
            spread[...],
            jnp.concatenate([one_hot, one_hot], axis=1),
            (((1,), (1,)), ((), ())),
            preferred_element_type=F32,
        )

        @pl.when(i == 0)
        def _():
            for g in range(CELLS // TILE):
                flux[:, g * TILE : (g + 1) * TILE] = landed[SURF * g : SURF * (g + 1)]

        @pl.when(i > 0)
        def _():
            for g in range(CELLS // TILE):
                flux[:, g * TILE : (g + 1) * TILE] += landed[SURF * g : SURF * (g + 1)]

    finish = pltpu.make_async_copy(flux, surface_flux, store_sem.at[1])
    finish.start()
    store.wait()
    finish.wait()


def local(*args):
    hbm = pl.BlockSpec(memory_space=pltpu.HBM)
    vmem = pl.BlockSpec(memory_space=pltpu.VMEM)
    second, incoming, target = pl.pallas_call(
        kernel,
        out_shape=(
            pltpu.VMEM((ROWS, CELLS), F32),
            pltpu.VMEM((3, SURF, SLOTS), F32),
            pltpu.VMEM((3, SLOTS), jnp.int32),
        ),
        in_specs=[hbm] * 8,
        out_specs=(vmem, vmem, vmem),
        scratch_shapes=[
            pltpu.VMEM((ROWS, WIDE), F32),
            pltpu.VMEM((NBR, NEAR), jnp.int32),
            pltpu.VMEM((NBR, NEAR), F32),
            pltpu.VMEM((ROWS, 3 * ROWS), BF16),
            pltpu.VMEM((ROWS, WIDE), F32),
            pltpu.VMEM((2 * ROWS, WIDE), BF16),
            pltpu.VMEM((NEAR // BLOCK // 2, 2, WINDOW, TILE), BF16),
            pltpu.VMEM((NEAR // BLOCK // 2, 2, WINDOW, TILE), BF16),
            pltpu.VMEM((NEAR // BLOCK // 2, 2, WINDOW, TILE), BF16),
            pltpu.VMEM((NEAR // BLOCK // 2, 2, WINDOW, TILE), BF16),
            pltpu.VMEM((ROWS, NEAR), F32),
            pltpu.VMEM((2 * ROWS, NEAR), BF16),
            pltpu.VMEM((3, SURF, SLOTS), F32),
            pltpu.VMEM((SURF * CELLS // TILE, 2 * TILE), BF16),
            pltpu.VMEM((1, ROWS, ROWS), F32),
            pltpu.VMEM((3, SLOTS), jnp.int32),
            pltpu.VMEM((3, SLOTS), F32),
            pltpu.SMEM((1, 3), jnp.int32),
            pltpu.SemaphoreType.DMA((8,)),
            pltpu.SemaphoreType.DMA((6,)),
            pltpu.SemaphoreType.DMA((6,)),
            pltpu.SemaphoreType.DMA((3, 2)),
            pltpu.SemaphoreType.DMA((3, 2)),
        ],
        compiler_params=pltpu.CompilerParams(
            collective_id=0, has_side_effects=True, vmem_limit_bytes=124 << 19
        ),
        name="coupled_update",
    )(*args)
    return pl.pallas_call(
        landing,
        out_shape=(
            jax.ShapeDtypeStruct((ROWS, CELLS), F32),
            jax.ShapeDtypeStruct((SURF, CELLS), F32),
        ),
        in_specs=[vmem] * 3,
        out_specs=(hbm, hbm),
        scratch_shapes=[
            pltpu.VMEM((SURF * CELLS // TILE, 2 * SLOTS), BF16),
            pltpu.VMEM((SURF, CELLS), F32),
            pltpu.SemaphoreType.DMA((2,)),
        ],
        compiler_params=pltpu.CompilerParams(vmem_limit_bytes=24 << 20),
        name="landing",
    )(second, incoming, target)


def solution(mesh):
    placed = (
        P(None, ("comp", "tile")),
        P(None, ("comp", "tile")),
        P(None, ("comp", "tile")),
        P("comp", None, None),
        P(("comp", "tile"), None),
        P(("comp", "tile"), None),
        P(("comp", "tile"), None),
        P(("comp", "tile"), None),
    )
    return jax.shard_map(
        local,
        mesh=mesh,
        in_specs=placed,
        out_specs=(P(None, ("comp", "tile")), P(None, ("comp", "tile"))),
        check_vma=False,
    )
```

```python
import jax
import jax.numpy as jnp
from jax import lax
from jax.experimental import pallas as pl
from jax.experimental.pallas import tpu as pltpu
from jax.sharding import PartitionSpec as P

ROWS = 80
SURF = 16
REST = ROWS - SURF
NBR = 8
CELLS = 4096
HALO = 256
SLOTS = 1024
TILE = 128
BLOCK = 256
WINDOW = TILE + 2 * HALO
SPAN = BLOCK + 2 * HALO
NEAR = CELLS + 2 * HALO
WIDE = CELLS + 4 * HALO
HALF = SLOTS // 2
OCEAN_X = 3
BF16 = jnp.bfloat16
F32 = jnp.float32
MESH = pl.DeviceIdType.MESH


def halves(value):
    high = value.astype(BF16)
    return high, (value - high.astype(F32)).astype(BF16)


def put_halves(ref, column, width, value):
    high, low = halves(value)
    columns = pl.ds(column, width)
    ref[0:SURF, columns] = high[:SURF]
    ref[SURF : 2 * SURF, columns] = low[:SURF]
    ref[2 * SURF : 2 * SURF + REST, columns] = high[SURF:]
    ref[2 * SURF + REST :, columns] = low[SURF:]


def row_of(ref, row, columns):
    second_or_third = jnp.where(row == 1, ref[1:2, columns], ref[2:3, columns])
    return jnp.where(row == 0, ref[0:1, columns], second_or_third)


def build_block(block, offset_ref, weight_ref, high_ref, low_ref, slot):
    for side in range(2):
        columns = pl.ds(pl.multiple_of(block * BLOCK + side * TILE, TILE), TILE)
        offset = offset_ref[:, columns]
        weight = weight_ref[:, columns]
        total = weight
        for shift in range(1, NBR):
            same = pltpu.roll(offset, shift, 0) == offset
            total = total + jnp.where(same, pltpu.roll(weight, shift, 0), 0.0)
        place = offset + HALO + lax.broadcasted_iota(jnp.int32, (NBR, TILE), 1)
        high, low = halves(total)
        high, low = high.astype(F32), low.astype(F32)
        places, highs, lows = [], [], []
        for k in range(NBR):
            places.append(jnp.broadcast_to(place[k : k + 1], (16, TILE)).astype(jnp.int16))
            highs.append(jnp.broadcast_to(high[k : k + 1], (16, TILE)).astype(BF16))
            lows.append(jnp.broadcast_to(low[k : k + 1], (16, TILE)).astype(BF16))
        row = lax.broadcasted_iota(jnp.int16, (16, TILE), 0)
        for r in range(WINDOW // 16):
            here = row + jnp.int16(16 * r)
            a = jnp.zeros((16, TILE), BF16)
            b = jnp.zeros((16, TILE), BF16)
            for k in range(NBR):
                hit = places[k] == here
                a = jnp.where(hit, highs[k], a)
                b = jnp.where(hit, lows[k], b)
            high_ref[slot, side, 16 * r : 16 * r + 16, :] = a
            low_ref[slot, side, 16 * r : 16 * r + 16, :] = b


def matrix(ref, slot):
    blank = jnp.zeros((TILE, TILE), BF16)
    left = jnp.concatenate([ref[slot, 0], blank], axis=0)
    right = jnp.concatenate([blank, ref[slot, 1]], axis=0)
    return jnp.concatenate([left, right], axis=1)


def kernel(
    fields,
    offsets,
    weights,
    vertical_in,
    source_in,
    share_in,
    count_in,
    target_in,
    second,
    incoming,
    target,
    raw,
    near_offset,
    near_weight,
    mix_ref,
    mixed,
    mixed_halves,
    even_high,
    even_low,
    odd_high,
    odd_low,
    first,
    first_halves,
    outgoing,
    surface_halves,
    vertical,
    source,
    share,
    count,
    local_sem,
    send_sem,
    recv_sem,
    packet_send,
    packet_recv,
):
    comp = lax.axis_index("comp")
    tile = lax.axis_index("tile")
    tiles = lax.axis_size("tile")
    column = comp // 2
    core = comp % 2
    is_ocean = column == OCEAN_X
    left = lax.rem(tile + tiles - 1, tiles)
    right = lax.rem(tile + 1, tiles)

    loads = []
    for ref, place in (
        (offsets, near_offset.at[:, pl.ds(HALO, CELLS)]),
        (weights, near_weight.at[:, pl.ds(HALO, CELLS)]),
        (vertical_in, vertical),
        (fields, raw.at[:, pl.ds(2 * HALO, CELLS)]),
        (source_in, source),
        (share_in, share),
        (count_in, count),
        (target_in, target),
    ):
        loads.append(pltpu.make_async_copy(ref, place, local_sem.at[len(loads)]))
        loads[-1].start()

    barrier = pltpu.get_barrier_semaphore()
    for side in (left, right):
        pl.semaphore_signal(barrier, inc=1, device_id=(comp, side), device_id_type=MESH)

    @pl.when(is_ocean)
    def _():
        for x in range(OCEAN_X):
            pl.semaphore_signal(barrier, inc=1, device_id=(2 * x + core, tile), device_id_type=MESH)

    @pl.when(jnp.logical_not(is_ocean))
    def _():
        pl.semaphore_signal(
            barrier, inc=1, device_id=(2 * OCEAN_X + core, tile), device_id_type=MESH
        )

    def edges(ref, near, width, base):
        ahead = pltpu.make_async_remote_copy(
            src_ref=ref.at[:, pl.ds(CELLS - width, width)],
            dst_ref=near.at[:, pl.ds(0, width)],
            send_sem=send_sem.at[base],
            recv_sem=recv_sem.at[base],
            device_id=(comp, right),
            device_id_type=MESH,
        )
        back = pltpu.make_async_remote_copy(
            src_ref=ref.at[:, pl.ds(0, width)],
            dst_ref=near.at[:, pl.ds(width + CELLS, width)],
            send_sem=send_sem.at[base + 1],
            recv_sem=recv_sem.at[base + 1],
            device_id=(comp, left),
            device_id_type=MESH,
        )
        return [ahead, back]

    halo = edges(fields, raw, 2 * HALO, 4)
    halo += edges(offsets, near_offset, HALO, 0)
    halo += edges(weights, near_weight, HALO, 2)
    loads[0].wait()
    loads[1].wait()

    highs_by = (even_high, odd_high)
    lows_by = (even_low, odd_low)

    def build(block, parity, slot):
        build_block(
            block, near_offset, near_weight, highs_by[parity], lows_by[parity], slot
        )

    build(1, 1, 0)
    build(2, 0, 1)
    loads[2].wait()

    own = vertical[0]
    rows = lax.broadcasted_iota(jnp.int32, (ROWS, ROWS), 0)
    columns = lax.broadcasted_iota(jnp.int32, (ROWS, ROWS), 1)
    unit = jnp.where(rows == columns, 1.0, 0.0).astype(F32)
    twice = unit + 2.0 * own + jnp.dot(own, own, precision=lax.Precision.HIGHEST)
    twice_high, twice_low = halves(twice)
    mix_ref[...] = jnp.concatenate(
        [twice_high.astype(F32), twice_high.astype(F32), twice_low.astype(F32)], axis=1
    ).astype(BF16)

    def mix(block):
        start = pl.multiple_of(block * BLOCK, BLOCK)
        high, low = halves(raw[:, pl.ds(start, BLOCK)])
        value = jnp.dot(
            mix_ref[...],
            jnp.concatenate([high, low, high], axis=0),
            preferred_element_type=F32,
        )
        mixed[:, pl.ds(start, BLOCK)] = value
        put_halves(mixed_halves, start, BLOCK, value)

    def centre(start):
        return 1.0 - jnp.sum(near_weight[:, pl.ds(start, BLOCK)], axis=0, keepdims=True)

    def first_update(block, parity, slot):
        start = pl.multiple_of(block * BLOCK, BLOCK)
        window = mixed_halves[:, pl.ds(start, SPAN)]
        highs = jnp.concatenate([window[:SURF], window[2 * SURF : 2 * SURF + REST]], axis=0)
        by_high = jnp.dot(window, matrix(highs_by[parity], slot), preferred_element_type=F32)
        by_low = jnp.dot(highs, matrix(lows_by[parity], slot), preferred_element_type=F32)
        surf = by_high[:SURF] + by_high[SURF : 2 * SURF]
        rest = by_high[2 * SURF : 2 * SURF + REST] + by_high[2 * SURF + REST :]
        moved = jnp.concatenate([surf, rest], axis=0) + by_low
        here = mixed[:, pl.ds(pl.multiple_of(start + HALO, BLOCK), BLOCK)]
        value = centre(start) * here + moved
        first[:, pl.ds(start, BLOCK)] = value
        put_halves(first_halves, start, BLOCK, value)

    loads[3].wait()
    for block in (2, 3, 4):
        mix(block)

    def second_update(pair, parity, row, height, half_row):
        start = pl.multiple_of((2 * pair + parity) * BLOCK, BLOCK)
        inner = pl.multiple_of(start + HALO, BLOCK)
        window = first_halves[half_row : half_row + 2 * height, pl.ds(start, SPAN)]
        slot = pair + parity
        by_high = jnp.dot(
            window, matrix(highs_by[1 - parity], slot), preferred_element_type=F32
        )
        by_low = jnp.dot(
            window[:height], matrix(lows_by[1 - parity], slot), preferred_element_type=F32
        )
        moved = by_high[:height] + by_high[height:] + by_low
        second[row : row + height, pl.ds(start, BLOCK)] = (
            centre(inner) * first[row : row + height, pl.ds(inner, BLOCK)] + moved
        )

    last = CELLS // BLOCK

    def fused(pairs, with_surface):
        @pl.loop(*pairs)
        def _(pair):
            for parity in range(2):
                block = 2 * pair + parity
                if with_surface:
                    second_update(pair - 2 + parity, 1 - parity, 0, SURF, 0)
                first_update(block, parity, pair)
                build(block + 1, 1 - parity, pair + parity)
                mix(block + 3)

    def surface(block):
        second_update(block // 2, block % 2, 0, SURF, 0)

    @pl.when(is_ocean)
    def _():
        pl.semaphore_wait(barrier, 2 + OCEAN_X)

    @pl.when(jnp.logical_not(is_ocean))
    def _():
        pl.semaphore_wait(barrier, 3)

    for copy in halo:
        copy.start()
    fused((1, 3), False)
    fused((3, last // 2 - 1), True)
    first_update(last - 2, 0, last // 2 - 1)
    surface(last - 5)
    build(last - 1, 1, last // 2 - 1)
    mix(last + 1)
    first_update(last - 1, 1, last // 2 - 1)
    surface(last - 4)
    build(last, 0, last // 2)
    for copy in halo:
        copy.wait()
    for block in (last + 2, last + 3, 0, 1):
        mix(block)
    first_update(last, 0, last // 2)
    surface(last - 3)
    build(last + 1, 1, last // 2)
    first_update(last + 1, 1, last // 2)
    surface(last - 2)
    build(0, 0, 0)
    surface(last - 1)
    first_update(0, 0, 0)
    first_update(1, 1, 0)
    for block in range(3):
        surface(block)

    for g in range(CELLS // TILE):
        high, low = halves(second[0:SURF, g * TILE : (g + 1) * TILE])
        surface_halves[SURF * g : SURF * (g + 1), 0:TILE] = high
        surface_halves[SURF * g : SURF * (g + 1), TILE:] = low

    for load in loads[4:]:
        load.wait()

    packets = jnp.where(is_ocean, 3, 1)

    def packet_copies(i):
        row = jnp.where(is_ocean, jnp.where(i == 2, 2, 1 - i), 2 - column)
        to = jnp.where(is_ocean, row, OCEAN_X)
        slot = jnp.where(is_ocean, 0, row)
        return row, [
            pltpu.make_async_remote_copy(
                src_ref=outgoing.at[i, :, pl.ds(half * HALF, HALF)],
                dst_ref=incoming.at[slot, :, pl.ds(half * HALF, HALF)],
                send_sem=packet_send.at[i, half],
                recv_sem=packet_recv.at[slot, half],
                device_id=(2 * to + core, tile),
                device_id_type=MESH,
            )
            for half in range(2)
        ]

    @pl.loop(0, packets)
    def _(i):
        row, copies = packet_copies(i)
        live = count[0, row]
        for half, copy in enumerate(copies):

            @pl.loop(half * HALF // BLOCK, (half + 1) * HALF // BLOCK, unroll=True)
            def _(p):
                start = pl.multiple_of(p * BLOCK, BLOCK)
                columns = pl.ds(start, BLOCK)
                place = row_of(source, row, columns)
                lane = jnp.bitwise_and(place, TILE - 1)
                lanes = lax.broadcasted_iota(jnp.int32, (TILE, BLOCK), 0)
                one_hot = jnp.where(lanes == lane, 1.0, 0.0).astype(BF16)
                got = jnp.dot(
                    surface_halves[...],
                    jnp.concatenate([one_hot, one_hot], axis=0),
                    preferred_element_type=F32,
                )
                group = jnp.broadcast_to(jnp.right_shift(place, 7), (SURF, BLOCK))
                slot = start + lax.broadcasted_iota(jnp.int32, (SURF, BLOCK), 1)
                factor = jnp.where(slot < live, row_of(share, row, columns), 0.0)
                picked = jnp.zeros((SURF, BLOCK), F32)
                for g in range(CELLS // TILE):
                    picked = jnp.where(group == g, got[SURF * g : SURF * (g + 1)], picked)
                outgoing[i, :, columns] = picked * factor

            copy.start()

    @pl.loop(0, last // 2)
    def _(pair):
        for parity in range(2):
            second_update(pair, parity, SURF, REST, 2 * SURF)

    @pl.loop(0, packets)
    def _(i):
        for half in range(2):
            part = incoming.at[i, :, pl.ds(half * HALF, HALF)]
            pltpu.make_async_copy(part, part, packet_recv.at[i, half]).wait()
            part = outgoing.at[i, :, pl.ds(half * HALF, HALF)]
            pltpu.make_async_copy(part, part, packet_send.at[i, half]).wait()


def landing(second, incoming, target, new_fields, surface_flux, spread, flux, store_sem):
    comp = lax.axis_index("comp")
    column = comp // 2
    is_ocean = column == OCEAN_X
    store = pltpu.make_async_copy(second, new_fields, store_sem.at[0])
    store.start()

    @pl.loop(0, jnp.where(is_ocean, 3, 1))
    def _(i):
        row = jnp.where(is_ocean, i, column)
        place = row_of(target, row, slice(None))
        lane = jnp.broadcast_to(jnp.bitwise_and(place, BLOCK - 1), (16, SLOTS)).astype(jnp.int16)
        group = jnp.broadcast_to(jnp.right_shift(place, 8), (16, SLOTS)).astype(jnp.int16)
        near = lax.broadcasted_iota(jnp.int16, (16, SLOTS), 0)
        one = jnp.ones((16, SLOTS), BF16)
        high, low = halves(incoming[i])
        zero = jnp.zeros((SURF, SLOTS), BF16)
        one_hot = jnp.concatenate(
            [jnp.where(lane == near + jnp.int16(16 * r), one, zero) for r in range(BLOCK // 16)],
            axis=0,
        )
        for g in range(CELLS // BLOCK):
            hit = group == jnp.int16(g)
            spread[SURF * g : SURF * (g + 1), 0:SLOTS] = jnp.where(hit, high, zero)
            spread[SURF * g : SURF * (g + 1), SLOTS:] = jnp.where(hit, low, zero)
        landed = lax.dot_general(
            spread[...],
            jnp.concatenate([one_hot, one_hot], axis=1),
            (((1,), (1,)), ((), ())),
            preferred_element_type=F32,
        )

        @pl.when(i == 0)
        def _():
            for g in range(CELLS // BLOCK):
                flux[:, g * BLOCK : (g + 1) * BLOCK] = landed[SURF * g : SURF * (g + 1)]

        @pl.when(i > 0)
        def _():
            for g in range(CELLS // BLOCK):
                flux[:, g * BLOCK : (g + 1) * BLOCK] += landed[SURF * g : SURF * (g + 1)]

    finish = pltpu.make_async_copy(flux, surface_flux, store_sem.at[1])
    finish.start()
    store.wait()
    finish.wait()


def local(*args):
    hbm = pl.BlockSpec(memory_space=pltpu.HBM)
    vmem = pl.BlockSpec(memory_space=pltpu.VMEM)
    second, incoming, target = pl.pallas_call(
        kernel,
        out_shape=(
            pltpu.VMEM((ROWS, CELLS), F32),
            pltpu.VMEM((3, SURF, SLOTS), F32),
            pltpu.VMEM((3, SLOTS), jnp.int32),
        ),
        in_specs=[hbm] * 8,
        out_specs=(vmem, vmem, vmem),
        scratch_shapes=[
            pltpu.VMEM((ROWS, WIDE), F32),
            pltpu.VMEM((NBR, NEAR), jnp.int32),
            pltpu.VMEM((NBR, NEAR), F32),
            pltpu.VMEM((ROWS, 3 * ROWS), BF16),
            pltpu.VMEM((ROWS, WIDE), F32),
            pltpu.VMEM((2 * ROWS, WIDE), BF16),
            pltpu.VMEM((NEAR // BLOCK // 2, 2, WINDOW, TILE), BF16),
            pltpu.VMEM((NEAR // BLOCK // 2, 2, WINDOW, TILE), BF16),
            pltpu.VMEM((NEAR // BLOCK // 2, 2, WINDOW, TILE), BF16),
            pltpu.VMEM((NEAR // BLOCK // 2, 2, WINDOW, TILE), BF16),
            pltpu.VMEM((ROWS, NEAR), F32),
            pltpu.VMEM((2 * ROWS, NEAR), BF16),
            pltpu.VMEM((3, SURF, SLOTS), F32),
            pltpu.VMEM((SURF * CELLS // TILE, 2 * TILE), BF16),
            pltpu.VMEM((1, ROWS, ROWS), F32),
            pltpu.VMEM((3, SLOTS), jnp.int32),
            pltpu.VMEM((3, SLOTS), F32),
            pltpu.SMEM((1, 3), jnp.int32),
            pltpu.SemaphoreType.DMA((8,)),
            pltpu.SemaphoreType.DMA((6,)),
            pltpu.SemaphoreType.DMA((6,)),
            pltpu.SemaphoreType.DMA((3, 2)),
            pltpu.SemaphoreType.DMA((3, 2)),
        ],
        compiler_params=pltpu.CompilerParams(
            collective_id=0, has_side_effects=True, vmem_limit_bytes=124 << 19
        ),
        name="coupled_update",
    )(*args)
    return pl.pallas_call(
        landing,
        out_shape=(
            jax.ShapeDtypeStruct((ROWS, CELLS), F32),
            jax.ShapeDtypeStruct((SURF, CELLS), F32),
        ),
        in_specs=[vmem] * 3,
        out_specs=(hbm, hbm),
        scratch_shapes=[
            pltpu.VMEM((SURF * CELLS // BLOCK, 2 * SLOTS), BF16),
            pltpu.VMEM((SURF, CELLS), F32),
            pltpu.SemaphoreType.DMA((2,)),
        ],
        compiler_params=pltpu.CompilerParams(vmem_limit_bytes=24 << 20),
        name="landing",
    )(second, incoming, target)


def solution(mesh):
    placed = (
        P(None, ("comp", "tile")),
        P(None, ("comp", "tile")),
        P(None, ("comp", "tile")),
        P("comp", None, None),
        P(("comp", "tile"), None),
        P(("comp", "tile"), None),
        P(("comp", "tile"), None),
        P(("comp", "tile"), None),
    )
    return jax.shard_map(
        local,
        mesh=mesh,
        in_specs=placed,
        out_specs=(P(None, ("comp", "tile")), P(None, ("comp", "tile"))),
        check_vma=False,
    )
```

```python
import jax
import jax.numpy as jnp
from jax import lax
from jax.experimental import pallas as pl
from jax.experimental.pallas import tpu as pltpu
from jax.sharding import PartitionSpec as P

ROWS = 80
SURF = 16
REST = ROWS - SURF
NBR = 8
CELLS = 4096
HALO = 256
SLOTS = 1024
TILE = 128
BLOCK = 256
WINDOW = TILE + 2 * HALO
SPAN = BLOCK + 2 * HALO
NEAR = CELLS + 2 * HALO
WIDE = CELLS + 4 * HALO
HALF = SLOTS // 2
OCEAN_X = 3
BF16 = jnp.bfloat16
F32 = jnp.float32
MESH = pl.DeviceIdType.MESH


def halves(value):
    high = value.astype(BF16)
    return high, (value - high.astype(F32)).astype(BF16)


def put_halves(ref, column, width, value):
    high, low = halves(value)
    columns = pl.ds(column, width)
    ref[0:SURF, columns] = high[:SURF]
    ref[SURF : 2 * SURF, columns] = low[:SURF]
    ref[2 * SURF : 2 * SURF + REST, columns] = high[SURF:]
    ref[2 * SURF + REST :, columns] = low[SURF:]


def row_of(ref, row, columns):
    second_or_third = jnp.where(row == 1, ref[1:2, columns], ref[2:3, columns])
    return jnp.where(row == 0, ref[0:1, columns], second_or_third)


def build_block(block, offset_ref, weight_ref, high_ref, low_ref, slot):
    for side in range(2):
        columns = pl.ds(pl.multiple_of(block * BLOCK + side * TILE, TILE), TILE)
        offset = offset_ref[:, columns]
        weight = weight_ref[:, columns]
        total = weight
        for shift in range(1, NBR):
            same = pltpu.roll(offset, shift, 0) == offset
            total = total + jnp.where(same, pltpu.roll(weight, shift, 0), 0.0)
        place = offset + HALO + lax.broadcasted_iota(jnp.int32, (NBR, TILE), 1)
        high, low = halves(total)
        high, low = high.astype(F32), low.astype(F32)
        places, highs, lows = [], [], []
        for k in range(NBR):
            places.append(jnp.broadcast_to(place[k : k + 1], (16, TILE)).astype(jnp.int16))
            highs.append(jnp.broadcast_to(high[k : k + 1], (16, TILE)).astype(BF16))
            lows.append(jnp.broadcast_to(low[k : k + 1], (16, TILE)).astype(BF16))
        row = lax.broadcasted_iota(jnp.int16, (16, TILE), 0)
        for r in range(WINDOW // 16):
            here = row + jnp.int16(16 * r)
            a = jnp.zeros((16, TILE), BF16)
            b = jnp.zeros((16, TILE), BF16)
            for k in range(NBR):
                hit = places[k] == here
                a = jnp.where(hit, highs[k], a)
                b = jnp.where(hit, lows[k], b)
            high_ref[slot, side, 16 * r : 16 * r + 16, :] = a
            low_ref[slot, side, 16 * r : 16 * r + 16, :] = b


def matrix(ref, slot):
    blank = jnp.zeros((TILE, TILE), BF16)
    left = jnp.concatenate([ref[slot, 0], blank], axis=0)
    right = jnp.concatenate([blank, ref[slot, 1]], axis=0)
    return jnp.concatenate([left, right], axis=1)


def kernel(
    fields,
    offsets,
    weights,
    vertical_in,
    source_in,
    share_in,
    count_in,
    target_in,
    second,
    incoming,
    target,
    raw,
    near_offset,
    near_weight,
    mix_ref,
    mixed,
    mixed_halves,
    even_high,
    even_low,
    odd_high,
    odd_low,
    first,
    first_halves,
    outgoing,
    surface_halves,
    vertical,
    source,
    share,
    count,
    local_sem,
    send_sem,
    recv_sem,
    packet_send,
    packet_recv,
):
    comp = lax.axis_index("comp")
    tile = lax.axis_index("tile")
    tiles = lax.axis_size("tile")
    column = comp // 2
    core = comp % 2
    is_ocean = column == OCEAN_X
    left = lax.rem(tile + tiles - 1, tiles)
    right = lax.rem(tile + 1, tiles)

    loads = []
    for ref, place in (
        (offsets, near_offset.at[:, pl.ds(HALO, CELLS)]),
        (weights, near_weight.at[:, pl.ds(HALO, CELLS)]),
        (vertical_in, vertical),
        (fields, raw.at[:, pl.ds(2 * HALO, CELLS)]),
        (source_in, source),
        (share_in, share),
        (count_in, count),
        (target_in, target),
    ):
        loads.append(pltpu.make_async_copy(ref, place, local_sem.at[len(loads)]))
        loads[-1].start()

    barrier = pltpu.get_barrier_semaphore()
    for side in (left, right):
        pl.semaphore_signal(barrier, inc=1, device_id=(comp, side), device_id_type=MESH)

    @pl.when(is_ocean)
    def _():
        for x in range(OCEAN_X):
            pl.semaphore_signal(barrier, inc=1, device_id=(2 * x + core, tile), device_id_type=MESH)

    @pl.when(jnp.logical_not(is_ocean))
    def _():
        pl.semaphore_signal(
            barrier, inc=1, device_id=(2 * OCEAN_X + core, tile), device_id_type=MESH
        )

    def edges(ref, near, width, base):
        ahead = pltpu.make_async_remote_copy(
            src_ref=ref.at[:, pl.ds(CELLS - width, width)],
            dst_ref=near.at[:, pl.ds(0, width)],
            send_sem=send_sem.at[base],
            recv_sem=recv_sem.at[base],
            device_id=(comp, right),
            device_id_type=MESH,
        )
        back = pltpu.make_async_remote_copy(
            src_ref=ref.at[:, pl.ds(0, width)],
            dst_ref=near.at[:, pl.ds(width + CELLS, width)],
            send_sem=send_sem.at[base + 1],
            recv_sem=recv_sem.at[base + 1],
            device_id=(comp, left),
            device_id_type=MESH,
        )
        return [ahead, back]

    halo = edges(fields, raw, 2 * HALO, 4)
    halo += edges(offsets, near_offset, HALO, 0)
    halo += edges(weights, near_weight, HALO, 2)
    loads[0].wait()
    loads[1].wait()

    highs_by = (even_high, odd_high)
    lows_by = (even_low, odd_low)

    def build(block, parity, slot):
        build_block(
            block, near_offset, near_weight, highs_by[parity], lows_by[parity], slot
        )

    build(1, 1, 0)
    build(2, 0, 1)
    loads[2].wait()

    own = vertical[0]
    rows = lax.broadcasted_iota(jnp.int32, (ROWS, ROWS), 0)
    columns = lax.broadcasted_iota(jnp.int32, (ROWS, ROWS), 1)
    unit = jnp.where(rows == columns, 1.0, 0.0).astype(F32)
    twice = unit + 2.0 * own + jnp.dot(own, own, precision=lax.Precision.HIGHEST)
    twice_high, twice_low = halves(twice)
    mix_ref[...] = jnp.concatenate(
        [twice_high.astype(F32), twice_high.astype(F32), twice_low.astype(F32)], axis=1
    ).astype(BF16)

    def mix(block):
        start = pl.multiple_of(block * BLOCK, BLOCK)
        high, low = halves(raw[:, pl.ds(start, BLOCK)])
        value = jnp.dot(
            mix_ref[...],
            jnp.concatenate([high, low, high], axis=0),
            preferred_element_type=F32,
        )
        mixed[:, pl.ds(start, BLOCK)] = value
        put_halves(mixed_halves, start, BLOCK, value)

    def centre(start):
        return 1.0 - jnp.sum(near_weight[:, pl.ds(start, BLOCK)], axis=0, keepdims=True)

    def first_update(block, parity, slot):
        start = pl.multiple_of(block * BLOCK, BLOCK)
        window = mixed_halves[:, pl.ds(start, SPAN)]
        highs = jnp.concatenate([window[:SURF], window[2 * SURF : 2 * SURF + REST]], axis=0)
        by_high = jnp.dot(window, matrix(highs_by[parity], slot), preferred_element_type=F32)
        by_low = jnp.dot(highs, matrix(lows_by[parity], slot), preferred_element_type=F32)
        surf = by_high[:SURF] + by_high[SURF : 2 * SURF]
        rest = by_high[2 * SURF : 2 * SURF + REST] + by_high[2 * SURF + REST :]
        moved = jnp.concatenate([surf, rest], axis=0) + by_low
        here = mixed[:, pl.ds(pl.multiple_of(start + HALO, BLOCK), BLOCK)]
        value = centre(start) * here + moved
        first[:, pl.ds(start, BLOCK)] = value
        put_halves(first_halves, start, BLOCK, value)

    loads[3].wait()
    for block in (2, 3, 4):
        mix(block)

    def second_update(pair, parity, row, height, half_row):
        start = pl.multiple_of((2 * pair + parity) * BLOCK, BLOCK)
        inner = pl.multiple_of(start + HALO, BLOCK)
        window = first_halves[half_row : half_row + 2 * height, pl.ds(start, SPAN)]
        slot = pair + parity
        by_high = jnp.dot(
            window, matrix(highs_by[1 - parity], slot), preferred_element_type=F32
        )
        by_low = jnp.dot(
            window[:height], matrix(lows_by[1 - parity], slot), preferred_element_type=F32
        )
        moved = by_high[:height] + by_high[height:] + by_low
        second[row : row + height, pl.ds(start, BLOCK)] = (
            centre(inner) * first[row : row + height, pl.ds(inner, BLOCK)] + moved
        )

    last = CELLS // BLOCK

    def fused(pairs, with_surface):
        @pl.loop(*pairs)
        def _(pair):
            for parity in range(2):
                block = 2 * pair + parity
                if with_surface:
                    second_update(pair - 2 + parity, 1 - parity, 0, SURF, 0)
                first_update(block, parity, pair)
                build(block + 1, 1 - parity, pair + parity)
                mix(block + 3)

    def surface(block):
        second_update(block // 2, block % 2, 0, SURF, 0)

    @pl.when(is_ocean)
    def _():
        pl.semaphore_wait(barrier, 2 + OCEAN_X)

    @pl.when(jnp.logical_not(is_ocean))
    def _():
        pl.semaphore_wait(barrier, 3)

    for copy in halo:
        copy.start()
    fused((1, 3), False)
    fused((3, last // 2 - 1), True)
    surface(last - 5)
    first_update(last - 2, 0, last // 2 - 1)
    build(last - 1, 1, last // 2 - 1)
    mix(last + 1)
    surface(last - 4)
    first_update(last - 1, 1, last // 2 - 1)
    build(last, 0, last // 2)
    for copy in halo:
        copy.wait()
    for block in (last + 2, last + 3, 0, 1):
        mix(block)
    surface(last - 3)
    first_update(last, 0, last // 2)
    surface(last - 2)
    build(last + 1, 1, last // 2)
    first_update(last + 1, 1, last // 2)
    build(0, 0, 0)
    surface(last - 1)
    first_update(0, 0, 0)
    first_update(1, 1, 0)
    for block in range(3):
        surface(block)

    for g in range(CELLS // TILE):
        high, low = halves(second[0:SURF, g * TILE : (g + 1) * TILE])
        surface_halves[SURF * g : SURF * (g + 1), 0:TILE] = high
        surface_halves[SURF * g : SURF * (g + 1), TILE:] = low

    for load in loads[4:]:
        load.wait()

    packets = jnp.where(is_ocean, 3, 1)

    def packet_copies(i):
        row = jnp.where(is_ocean, jnp.where(i == 2, 2, 1 - i), 2 - column)
        to = jnp.where(is_ocean, row, OCEAN_X)
        slot = jnp.where(is_ocean, 0, row)
        return row, [
            pltpu.make_async_remote_copy(
                src_ref=outgoing.at[i, :, pl.ds(half * HALF, HALF)],
                dst_ref=incoming.at[slot, :, pl.ds(half * HALF, HALF)],
                send_sem=packet_send.at[i, half],
                recv_sem=packet_recv.at[slot, half],
                device_id=(2 * to + core, tile),
                device_id_type=MESH,
            )
            for half in range(2)
        ]

    @pl.loop(0, packets)
    def _(i):
        row, copies = packet_copies(i)
        live = count[0, row]
        for half, copy in enumerate(copies):

            @pl.loop(half * HALF // BLOCK, (half + 1) * HALF // BLOCK, unroll=True)
            def _(p):
                start = pl.multiple_of(p * BLOCK, BLOCK)
                columns = pl.ds(start, BLOCK)
                place = row_of(source, row, columns)
                lane = jnp.bitwise_and(place, TILE - 1)
                lanes = lax.broadcasted_iota(jnp.int32, (TILE, BLOCK), 0)
                one_hot = jnp.where(lanes == lane, 1.0, 0.0).astype(BF16)
                got = jnp.dot(
                    surface_halves[...],
                    jnp.concatenate([one_hot, one_hot], axis=0),
                    preferred_element_type=F32,
                )
                group = jnp.broadcast_to(jnp.right_shift(place, 7), (SURF, BLOCK))
                slot = start + lax.broadcasted_iota(jnp.int32, (SURF, BLOCK), 1)
                factor = jnp.where(slot < live, row_of(share, row, columns), 0.0)
                picked = jnp.zeros((SURF, BLOCK), F32)
                for g in range(CELLS // TILE):
                    picked = jnp.where(group == g, got[SURF * g : SURF * (g + 1)], picked)
                outgoing[i, :, columns] = picked * factor

            copy.start()

    @pl.loop(0, last // 2)
    def _(pair):
        for parity in range(2):
            second_update(pair, parity, SURF, REST, 2 * SURF)

    @pl.loop(0, packets)
    def _(i):
        for half in range(2):
            part = incoming.at[i, :, pl.ds(half * HALF, HALF)]
            pltpu.make_async_copy(part, part, packet_recv.at[i, half]).wait()
            part = outgoing.at[i, :, pl.ds(half * HALF, HALF)]
            pltpu.make_async_copy(part, part, packet_send.at[i, half]).wait()


def landing(second, incoming, target, new_fields, surface_flux, spread, flux, store_sem):
    comp = lax.axis_index("comp")
    column = comp // 2
    is_ocean = column == OCEAN_X
    store = pltpu.make_async_copy(second, new_fields, store_sem.at[0])
    store.start()

    def land(i, row):
        place = row_of(target, row, slice(None))
        lane = jnp.broadcast_to(jnp.bitwise_and(place, BLOCK - 1), (16, SLOTS)).astype(jnp.int16)
        group = jnp.broadcast_to(jnp.right_shift(place, 8), (16, SLOTS)).astype(jnp.int16)
        near = lax.broadcasted_iota(jnp.int16, (16, SLOTS), 0)
        one = jnp.ones((16, SLOTS), BF16)
        high, low = halves(incoming[i])
        zero = jnp.zeros((SURF, SLOTS), BF16)
        one_hot = jnp.concatenate(
            [jnp.where(lane == near + jnp.int16(16 * r), one, zero) for r in range(BLOCK // 16)],
            axis=0,
        )
        for g in range(CELLS // BLOCK):
            hit = group == jnp.int16(g)
            spread[i, SURF * g : SURF * (g + 1), 0:SLOTS] = jnp.where(hit, high, zero)
            spread[i, SURF * g : SURF * (g + 1), SLOTS:] = jnp.where(hit, low, zero)
        return lax.dot_general(
            spread[i],
            jnp.concatenate([one_hot, one_hot], axis=1),
            (((1,), (1,)), ((), ())),
            preferred_element_type=F32,
        )

    def put(landed):
        for g in range(CELLS // BLOCK):
            flux[:, g * BLOCK : (g + 1) * BLOCK] = landed[SURF * g : SURF * (g + 1)]

    @pl.when(is_ocean)
    def _():
        put(land(0, 0) + land(1, 1) + land(2, 2))

    @pl.when(jnp.logical_not(is_ocean))
    def _():
        put(land(0, column))

    finish = pltpu.make_async_copy(flux, surface_flux, store_sem.at[1])
    finish.start()
    store.wait()
    finish.wait()


def local(*args):
    hbm = pl.BlockSpec(memory_space=pltpu.HBM)
    vmem = pl.BlockSpec(memory_space=pltpu.VMEM)
    second, incoming, target = pl.pallas_call(
        kernel,
        out_shape=(
            pltpu.VMEM((ROWS, CELLS), F32),
            pltpu.VMEM((3, SURF, SLOTS), F32),
            pltpu.VMEM((3, SLOTS), jnp.int32),
        ),
        in_specs=[hbm] * 8,
        out_specs=(vmem, vmem, vmem),
        scratch_shapes=[
            pltpu.VMEM((ROWS, WIDE), F32),
            pltpu.VMEM((NBR, NEAR), jnp.int32),
            pltpu.VMEM((NBR, NEAR), F32),
            pltpu.VMEM((ROWS, 3 * ROWS), BF16),
            pltpu.VMEM((ROWS, WIDE), F32),
            pltpu.VMEM((2 * ROWS, WIDE), BF16),
            pltpu.VMEM((NEAR // BLOCK // 2, 2, WINDOW, TILE), BF16),
            pltpu.VMEM((NEAR // BLOCK // 2, 2, WINDOW, TILE), BF16),
            pltpu.VMEM((NEAR // BLOCK // 2, 2, WINDOW, TILE), BF16),
            pltpu.VMEM((NEAR // BLOCK // 2, 2, WINDOW, TILE), BF16),
            pltpu.VMEM((ROWS, NEAR), F32),
            pltpu.VMEM((2 * ROWS, NEAR), BF16),
            pltpu.VMEM((3, SURF, SLOTS), F32),
            pltpu.VMEM((SURF * CELLS // TILE, 2 * TILE), BF16),
            pltpu.VMEM((1, ROWS, ROWS), F32),
            pltpu.VMEM((3, SLOTS), jnp.int32),
            pltpu.VMEM((3, SLOTS), F32),
            pltpu.SMEM((1, 3), jnp.int32),
            pltpu.SemaphoreType.DMA((8,)),
            pltpu.SemaphoreType.DMA((6,)),
            pltpu.SemaphoreType.DMA((6,)),
            pltpu.SemaphoreType.DMA((3, 2)),
            pltpu.SemaphoreType.DMA((3, 2)),
        ],
        compiler_params=pltpu.CompilerParams(
            collective_id=0, has_side_effects=True, vmem_limit_bytes=124 << 19
        ),
        name="coupled_update",
    )(*args)
    return pl.pallas_call(
        landing,
        out_shape=(
            jax.ShapeDtypeStruct((ROWS, CELLS), F32),
            jax.ShapeDtypeStruct((SURF, CELLS), F32),
        ),
        in_specs=[vmem] * 3,
        out_specs=(hbm, hbm),
        scratch_shapes=[
            pltpu.VMEM((3, SURF * CELLS // BLOCK, 2 * SLOTS), BF16),
            pltpu.VMEM((SURF, CELLS), F32),
            pltpu.SemaphoreType.DMA((2,)),
        ],
        compiler_params=pltpu.CompilerParams(vmem_limit_bytes=24 << 20),
        name="landing",
    )(second, incoming, target)


def solution(mesh):
    placed = (
        P(None, ("comp", "tile")),
        P(None, ("comp", "tile")),
        P(None, ("comp", "tile")),
        P("comp", None, None),
        P(("comp", "tile"), None),
        P(("comp", "tile"), None),
        P(("comp", "tile"), None),
        P(("comp", "tile"), None),
    )
    return jax.shard_map(
        local,
        mesh=mesh,
        in_specs=placed,
        out_specs=(P(None, ("comp", "tile")), P(None, ("comp", "tile"))),
        check_vma=False,
    )
```
